32 devices in a mesh: groups: 2 (over y), chan: 4 (over z), tm: 2 (over x), beam: 2 (over core).
Axes of the slice: x: 2, y: 2, z: 4, core: 2. Of those that a mesh axis runs over, the one named last changes fastest.
Arguments:
- voltages: bfloat16 [1024, 32768], P(('groups', 'chan', 'beam'), 'tm'), parts along dimension 0, may hold values from -6 to 6
- filter_taps: float32 [8, 1024], replicated, may hold values from -0.09375 to 0.09375
- beam_weights: bfloat16 [256, 2, 1024], replicated, may hold values from -0.25 to 0.25
- station_index: int32 [512], replicated, may hold values from 0 to 255, as said below
- delay_table: int32 [512, 8], P('chan'), may hold values from 0 to 32, as said below
Outputs:
- dedispersed: float32 [2048, 8, 32], P(('groups', 'chan', 'beam'), None, 'tm'), parts along dimension 0
The draws below stay inside these ranges and needn't reach their ends.
There are 2 independent parts, one for each index of `groups`. The reference program is written for one: setup_inputs(seed, part) draws one part's arguments, and reference() takes and returns one part's arrays. A program takes and returns all parts, laid end to end along the dimension named above; an argument that names none is the same for every part. Nothing has to cross between parts.
Inputs may be any that keep to these rules, and one draw needn't show every extreme that they name: `station_index`: the even inputs name each of the 256 weight rows once, and so do the odd inputs. `delay_table`: some entry equals 32.
All inputs are finite; a program needn't handle non-finite values.
Results may differ from the reference program's by a relative error of at most 0.0029.
Values may be sent and summed in bfloat16 or wider, within the bound.
A program may use at most 64 MiB of HBM per device.

```python
import math
import jax
import jax.numpy as jnp
from jax import lax

INPUTS = 512
STATIONS = 256
NFFT = 1024
CHANNELS = 512
TAPS = 8
BEAMS = 1024
NDM = 8
MAXD = 32
FRAMES = 32
SAMPLES = 32768


def draw_station_index(key, part):
    even_order = jax.random.permutation(jax.random.fold_in(key, 11), STATIONS).astype(jnp.int32)
    odd_order = jax.random.permutation(jax.random.fold_in(key, 12), STATIONS).astype(jnp.int32)
    return jnp.stack([even_order, odd_order], axis=1).reshape(INPUTS).astype(jnp.int32)


def draw_delay_table(key, part):
    table = jax.random.randint(jax.random.fold_in(key, 21), (CHANNELS, NDM), 0, MAXD + 1, dtype=jnp.int32)
    marked_row = jax.random.randint(jax.random.fold_in(key, 22), (), 0, CHANNELS, dtype=jnp.int32)
    marked_col = jax.random.randint(jax.random.fold_in(key, 23), (), 0, NDM, dtype=jnp.int32)
    row_match = jnp.arange(CHANNELS, dtype=jnp.int32)[:, None] == marked_row
    col_match = jnp.arange(NDM, dtype=jnp.int32)[None, :] == marked_col
    return jnp.where(row_match & col_match, MAXD, table).astype(jnp.int32)


def block_levels(stream_key, shape, split, low, largest):
    gain, own = 1.0, jax.random.fold_in(stream_key, 6)
    for axis_at, blocks in split:
        draws = jnp.exp(jax.random.uniform(jax.random.fold_in(own, axis_at), (blocks,), jnp.float32, low / len(split), largest / len(split)))
        gain = gain * jnp.repeat(draws, shape[axis_at] // blocks).reshape([-1 if axis == axis_at else 1 for axis in range(len(shape))])
    return gain


def bell_draw(key, dims, spread, bound, split=(), held_as=jnp.bfloat16):
    drawn = spread * jax.random.normal(key, dims, jnp.float32)
    if split:
        drawn = drawn * block_levels(key, dims, split, -0.22, 0.18)
    return jnp.clip(drawn, -bound, bound).astype(held_as)


def setup_inputs(seed: int = 0, part: int = 0) -> dict:
    keys = jax.random.split(jax.random.key(seed), 6)
    part_keys = jax.random.split(jax.random.fold_in(keys[5], part), 6)
    return {
        "voltages": bell_draw(part_keys[0], (INPUTS, SAMPLES), 1.0, 6.0, ((0, 8), (1, 2))),
        "filter_taps": bell_draw(keys[1], (TAPS, NFFT), (NFFT * TAPS // 2) ** -0.5, 0.09375, (), jnp.float32),
        "beam_weights": bell_draw(keys[2], (STATIONS, 2, BEAMS), INPUTS ** -0.5, 0.25),
        "station_index": draw_station_index(jax.random.fold_in(keys[5], 71), part),
        "delay_table": draw_delay_table(jax.random.fold_in(keys[5], 71), part),
    }


def dft_table(length):
    sample = jnp.arange(length, dtype=jnp.int32)
    column = jnp.arange(length // 2, dtype=jnp.int32)
    phase_index = sample[:, None] * column[None, :] % length
    angle_rad = phase_index.astype(jnp.float32) * (2.0 * math.pi / length)
    return jnp.stack([jnp.cos(angle_rad), -jnp.sin(angle_rad)], axis=1).astype(jnp.bfloat16)

def make_mixer(station_rows):
    real_part = station_rows[:, 0, :]
    imag_part = station_rows[:, 1, :]
    upper = jnp.concatenate([real_part, imag_part], axis=1)
    lower_half = jnp.concatenate([-imag_part, real_part], axis=1)
    return jnp.concatenate([upper, lower_half], axis=0)

def reference(voltages, filter_taps, beam_weights, station_index, delay_table):
    leading = jnp.zeros((INPUTS, (TAPS - 1) * NFFT), jnp.bfloat16)
    extended = jnp.concatenate([leading, voltages], axis=1).reshape(INPUTS, FRAMES + TAPS - 1, NFFT)
    filtered = jnp.zeros((INPUTS, FRAMES, NFFT), jnp.float32)
    for t in range(TAPS):
        filtered = filtered + filter_taps[t] * extended[:, t:t + FRAMES].astype(jnp.float32)
    filtered = filtered.astype(jnp.bfloat16)
    spectra = jnp.dot(filtered.reshape(INPUTS * FRAMES, NFFT), dft_table(NFFT).reshape(NFFT, NFFT), preferred_element_type=jnp.float32).astype(jnp.bfloat16)
    spectra = spectra.reshape(STATIONS, 2, FRAMES, 2, CHANNELS)
    pairs = station_index.reshape(STATIONS, 2)
    stacks = []
    mixers = []
    for p in range(2):
        stacks.append(jnp.transpose(spectra[:, p], (3, 1, 2, 0)).reshape(CHANNELS, FRAMES, 2 * STATIONS))
        mixers.append(make_mixer(beam_weights[pairs[:, p]]))

    def channel_power(pair_stacks):
        power_grid = jnp.zeros((FRAMES, BEAMS), jnp.float32)
        for p in range(2):
            voltage = jnp.dot(pair_stacks[p], mixers[p], preferred_element_type=jnp.float32)
            real_part = voltage[:, :BEAMS]
            imag_part = voltage[:, BEAMS:]
            power_grid = power_grid + real_part * real_part + imag_part * imag_part
        return power_grid
    power_grid = lax.map(channel_power, (stacks[0], stacks[1]))
    baseline = lax.optimization_barrier(jnp.sum(power_grid, axis=1)) / FRAMES
    excess = (power_grid - baseline[:, None, :]).astype(jnp.bfloat16)
    padded = jnp.pad(excess, ((0, 0), (0, MAXD), (0, 0)))
    channel_rows = jnp.arange(CHANNELS, dtype=jnp.int32)[:, None]
    offsets = jnp.arange(FRAMES, dtype=jnp.int32)[None, :]
    curves = []
    for d in range(NDM):
        picked = padded[channel_rows, delay_table[:, d][:, None] + offsets, :]
        curves.append(lax.optimization_barrier(jnp.sum(picked, axis=0, dtype=jnp.float32)))
    stacked_curves = jnp.transpose(jnp.stack(curves, axis=0), (2, 0, 1))
    return stacked_curves * (1.0 / math.sqrt(CHANNELS))
```

```python
import functools
import math

import jax
import jax.numpy as jnp
import numpy as np
from jax import lax
from jax.experimental import pallas as pl
from jax.experimental.pallas import tpu as pltpu
from jax.sharding import PartitionSpec as P

MAXD = 32
CHUNK = 4
MESH = pl.DeviceIdType.MESH


def shifted(value, axis, steps):
    count = lax.axis_size(axis)
    leading, last = (max(0, -steps), min(count, count - steps))
    return lax.ppermute(value, axis, [(source, source + steps) for source in range(leading, last)])


def dft_parts(length):
    phase = np.arange(length, dtype=np.int64)[:, None] * np.arange(length // 2, dtype=np.int64)[None, :] % length
    angle = phase.astype(np.float32) * np.float32(2.0 * math.pi / length)
    return np.stack([np.cos(angle), -np.sin(angle)], axis=1)


def chosen_rows(rows, station_index):
    hot = (station_index[:, None] == jnp.arange(rows.shape[0], dtype=jnp.int32)[None, :]).astype(rows.dtype)
    return jnp.dot(hot, rows, preferred_element_type=jnp.float32).astype(rows.dtype)


def make_mixer(real_part, imag_part):
    upper = jnp.concatenate([real_part, imag_part], axis=1)
    lower_half = jnp.concatenate([-imag_part, real_part], axis=1)
    return jnp.concatenate([upper, lower_half], axis=0)


def dedisperse(excess, delay_table, outputs):
    frame = jnp.arange(excess.shape[1], dtype=jnp.int32)
    offsets = jnp.arange(outputs, dtype=jnp.int32)
    wanted = delay_table[:, :, None] + offsets[None, None, :]
    hot = (wanted[:, :, :, None] == frame).astype(jnp.bfloat16)
    return jnp.einsum("kdog,kgb->bdo", hot, excess, preferred_element_type=jnp.float32)


def collective_shards(voltages, filter_taps, beam_weights, station_index, delay_table):
    tap_count, length = filter_taps.shape
    in_dev = voltages.shape[0]
    frames_dev = voltages.shape[1] // length
    chan_devices = lax.axis_size("chan")
    beam_devices = lax.axis_size("beam")
    time_devices = lax.axis_size("tm")
    history_rim = shifted(voltages[:, (frames_dev - tap_count + 1) * length :], "tm", 1)
    extended = jnp.concatenate([history_rim, voltages], axis=1).reshape(
        in_dev, frames_dev + tap_count - 1, length
    )
    filtered = jnp.zeros((in_dev, frames_dev, length), jnp.float32)
    for t in range(tap_count):
        filtered = filtered + filter_taps[t] * extended[:, t : t + frames_dev].astype(jnp.float32)
    filtered = filtered.astype(jnp.bfloat16).reshape(in_dev // 2, 2, frames_dev, length)
    table = jnp.asarray(dft_parts(length), jnp.bfloat16)
    spectra = jnp.einsum(
        "sqfn,nrk->kqrsf", filtered, table, preferred_element_type=jnp.float32
    ).astype(jnp.bfloat16)
    stations = beam_weights.shape[0]
    beams_local = beam_weights.shape[2] // beam_devices
    beam_share = beams_local // chan_devices
    arranged = beam_weights.reshape(stations, 2, chan_devices, beam_devices, beam_share)
    chosen = lax.dynamic_index_in_dim(arranged, lax.axis_index("beam"), 3, keepdims=False).reshape(
        stations, 2 * beams_local
    )
    station_order = jnp.transpose(
        station_index.reshape(chan_devices, beam_devices, in_dev // 2, 2), (3, 1, 0, 2)
    ).reshape(2, -1)
    mixers = []
    for p in range(2):
        rows = chosen_rows(chosen, station_order[p])
        mixers.append(make_mixer(rows[:, :beams_local], rows[:, beams_local:]))
    gathered = lax.all_gather(
        lax.all_to_all(spectra, "chan", split_axis=0, concat_axis=3, tiled=True),
        "beam",
        axis=3,
        tiled=True,
    )
    chan_count = gathered.shape[0]
    frames_here = gathered.shape[4]
    power_grid = jnp.zeros((chan_count, frames_here, beams_local), jnp.float32)
    for p in range(2):
        stacked = gathered[:, p].reshape(chan_count, -1, frames_here)
        voltage = jnp.einsum("kmf,mb->kfb", stacked, mixers[p], preferred_element_type=jnp.float32)
        real_part = voltage[:, :, :beams_local]
        imag_part = voltage[:, :, beams_local:]
        power_grid = power_grid + real_part * real_part + imag_part * imag_part
    frame_sums = lax.psum(jnp.sum(power_grid, axis=1), "tm")
    baseline = frame_sums / (frames_dev * time_devices)
    excess = (power_grid - baseline[:, None, :]).astype(jnp.bfloat16)
    devices_ahead = (MAXD + frames_dev - 1) // frames_dev
    pieces = [excess]
    for k in range(1, devices_ahead + 1):
        pieces.append(shifted(excess, "tm", -k))
    joined = jnp.concatenate(pieces, axis=1)
    summed = lax.psum_scatter(
        dedisperse(joined, delay_table, frames_dev), "chan", scatter_dimension=0, tiled=True
    )
    return summed * (1.0 / math.sqrt(length // 2))


def kernel(
    chips, frames, volt, taps, table, weights, order, delays, out,
    hist, mixed, filt, send, recv, xt, mix, power, exb, split, pick, lean,
    part, first, half, second, third_out, third,
    hist_sem, send_sem, recv_sem, tail_send, tail_recv,
):
    chan, tm, core = lax.axis_index("chan"), lax.axis_index("tm"), lax.axis_index("beam")
    tap_count, length = taps.shape
    rim = tap_count - 1
    inputs = volt.shape[0]
    per_pol = inputs // 2
    lanes = send.shape[-1]
    kk = lanes // 2
    curves = delays.shape[0]
    stations, wide = weights.shape
    beams = wide // 2
    me = chan * 2 + core
    other = 1 - core
    offsets = [o for o in (2, 1, 3) if o < chips] + [o for o in range(4, chips)] + [0]

    def at(oc):
        return lax.rem(chan + oc, chips)

    barrier = pltpu.get_barrier_semaphore()
    peers = 0
    for oc in range(chips):
        for db in range(2):
            if oc or db:
                pl.semaphore_signal(
                    barrier, inc=1, device_id={"chan": at(oc), "beam": lax.rem(core + db, 2)}, device_id_type=MESH
                )
                peers += 1
    pl.semaphore_signal(barrier, inc=1, device_id={"tm": 1 - tm}, device_id_type=MESH)
    pl.semaphore_wait(barrier, peers + 1)

    history = pltpu.make_async_remote_copy(
        src_ref=volt.at[:, pl.ds((frames - rim) * length, rim * length)],
        dst_ref=hist,
        send_sem=hist_sem.at[0],
        recv_sem=hist_sem.at[1],
        device_id={"tm": 1 - tm},
        device_id_type=MESH,
    )

    @pl.when(tm == 0)
    def _():
        history.start()
        hist[...] = jnp.zeros_like(hist)

    def corner(ci, f0, oc, db):
        target = lax.rem(core + db, 2)
        return pltpu.make_async_remote_copy(
            src_ref=send.at[ci, oc, target],
            dst_ref=recv.at[pl.ds(f0, CHUNK), :, me],
            send_sem=send_sem.at[ci, oc, db],
            recv_sem=recv_sem.at[ci, oc, db],
            device_id={"chan": at(oc), "beam": target},
            device_id_type=MESH,
        )

    def produce(ci, f0):
        @pl.loop(0, length // 128)
        def _(block):
            base = pl.multiple_of(block * 128, 128)
            for f in range(CHUNK):
                total = None
                for t in range(tap_count):
                    g = f0 + f - rim + t
                    if g < 0:
                        value = hist[:, pl.ds((g + rim) * length + base, 128)]
                    else:
                        value = volt[:, pl.ds(g * length + base, 128)]
                    term = taps[pl.ds(t, 1), pl.ds(base, 128)] * value.astype(jnp.float32)
                    total = term if total is None else total + term
                mixed[f] = total
                for p in range(2):
                    filt[f, p, :, pl.ds(base, 128)] = mixed[f, pl.ds(p, per_pol, stride=2), :].astype(jnp.bfloat16)

        rows = filt[...].reshape(CHUNK * inputs, length)
        for oc in offsets:
            slab = jnp.dot(rows, table[at(oc)], preferred_element_type=jnp.float32).astype(jnp.bfloat16)
            for b in range(2):
                send[ci, oc, b] = slab[:, b * lanes : (b + 1) * lanes].reshape(CHUNK, 2, per_pol, lanes)
            for db in range(2):
                if oc or db:
                    corner(ci, f0, oc, db).start()
        recv[pl.ds(f0, CHUNK), :, me] = send[ci, 0, core]

    def beamform(ci, f0):
        for oc in offsets:
            for db in range(2):
                if oc or db:
                    corner(ci, f0, oc, db).wait_recv()
        for f in range(CHUNK):
            for p in range(2):
                xt[p, f * lanes : (f + 1) * lanes, :] = recv[f0 + f, p].reshape(stations, lanes).T

        @pl.loop(0, beams // 256)
        def _(tile):
            base = pl.multiple_of(tile * 256, 256)
            for f in range(CHUNK):
                total = None
                for p in range(2):
                    rows = xt[p, f * lanes : (f + 1) * lanes, :]
                    by_real = jnp.dot(rows, mix[p, :, pl.ds(base, 256)], preferred_element_type=jnp.float32)
                    by_imag = jnp.dot(rows, mix[p, :, pl.ds(beams + base, 256)], preferred_element_type=jnp.float32)
                    real = by_real[:kk] - by_imag[kk:]
                    imag = by_imag[:kk] + by_real[kk:]
                    square = real * real + imag * imag
                    total = square if total is None else total + square
                power[f0 + f, :, pl.ds(base, 256)] = total

    def tables():
        station = lax.broadcasted_iota(jnp.int32, (stations, stations), 1)
        for p in range(2):
            hot = jnp.where(order[:, p : p + 1] == station, 1.0, 0.0).astype(jnp.bfloat16)
            for c in range(0, wide, 256):
                mix[p, :, c : c + 256] = jnp.dot(
                    hot, weights[:, c : c + 256], preferred_element_type=jnp.float32
                ).astype(jnp.bfloat16)
        for t in range(2):
            for d in range(curves):
                row = (t * curves + d) * frames
                wanted = t * frames + lax.broadcasted_iota(jnp.int32, (frames, frames * kk), 0) + delays[d : d + 1, :]
                here = tm * frames + lax.broadcasted_iota(jnp.int32, (frames, frames * kk), 1) // kk
                pick[row : row + frames, :] = jnp.where(wanted == here, 1.0, 0.0).astype(jnp.bfloat16)
                near = wanted[:, : 4 * kk]
                inside = jnp.where((near >= tm * frames) & (near < (tm + 1) * frames), 1.0, 0.0)
                valid = jnp.where(near < 2 * frames, 0.5, 0.0)
                lean[row : row + frames, :] = (inside - valid).astype(jnp.bfloat16)

    starts = [frames - CHUNK * (i + 1) for i in range(frames // CHUNK)]
    waited = False
    formed = 0
    for ci, f0 in enumerate(starts):
        if f0 < rim and not waited:
            waited = True
            tables()
            beamform(0, starts[0])
            formed = 1

            @pl.when(tm == 0)
            def _():
                history.wait_send()

            @pl.when(tm == 1)
            def _():
                history.wait_recv()

        produce(ci, f0)
    for ci in range(formed, len(starts)):
        beamform(ci, starts[ci])

    @pl.loop(0, beams // 128)
    def _(tile):
        base = pl.multiple_of(tile * 128, 128)
        block = power[:, :, pl.ds(base, 128)]
        mean = jnp.sum(block, axis=0) * (1.0 / frames)
        exb[:, pl.ds(base, 128)] = (block - mean[None]).reshape(frames * kk, 128).astype(jnp.bfloat16)
        high = mean.astype(jnp.bfloat16)
        rest = mean - high.astype(jnp.float32)
        middle = rest.astype(jnp.bfloat16)
        low = (rest - middle.astype(jnp.float32)).astype(jnp.bfloat16)
        split[:, pl.ds(base, 128)] = jnp.concatenate([high, middle, low, jnp.zeros_like(low)], axis=0)

    def tail(stage, oc, src, dst, target):
        return pltpu.make_async_remote_copy(
            src_ref=src,
            dst_ref=dst,
            send_sem=tail_send.at[stage, oc],
            recv_sem=tail_recv.at[stage, oc],
            device_id=target,
            device_id_type=MESH,
        )

    to_core, to_time, to_chip = {}, {}, {}
    rows = curves * frames
    for oc in offsets:
        base = pl.multiple_of(at(oc) * 256, 256)
        sums = jnp.dot(pick[...], exb[:, pl.ds(base, 256)], preferred_element_type=jnp.float32)
        sums = sums + jnp.dot(lean[...], split[:, pl.ds(base, 256)], preferred_element_type=jnp.float32)
        for b in range(2):
            for t in range(2):
                part[b, oc, t] = sums[t * rows : (t + 1) * rows, b * 128 : (b + 1) * 128]
        to_core[oc] = tail(0, oc, part.at[other, oc], first.at[oc], {"beam": other})
        to_core[oc].start()
    for oc in offsets:
        to_core[oc].wait_recv()
        half[oc] = part[core, oc] + first[oc]
        to_time[oc] = tail(1, oc, half.at[oc, 1 - tm], second.at[oc], {"tm": 1 - tm})
        to_time[oc].start()
    for oc in offsets:
        to_time[oc].wait_recv()
        third_out[oc] = half[oc, tm] + second[oc]
        if oc:
            to_chip[oc] = tail(2, oc, third_out.at[oc], third.at[oc], {"chan": at(oc)})
            to_chip[oc].start()
    total = third_out[0]
    for oc in offsets:
        if oc:
            to_chip[oc].wait_recv()
            total = total + third[oc]
    out[...] = total * (1.0 / math.sqrt(length // 2))
    for ci, f0 in enumerate(starts):
        for oc in offsets:
            for db in range(2):
                if oc or db:
                    corner(ci, f0, oc, db).wait_send()
    for copies in (to_core, to_time, to_chip):
        for copy in copies.values():
            copy.wait_send()


def kernel_shards(voltages, filter_taps, beam_weights, station_index, delay_table):
    length = filter_taps.shape[1]
    tap_count = filter_taps.shape[0]
    inputs = voltages.shape[0]
    frames = voltages.shape[1] // length
    chips = lax.axis_size("chan")
    stations, _, beams = beam_weights.shape
    curves = delay_table.shape[1]
    kk = delay_table.shape[0] // 2
    lanes = 2 * kk
    table = dft_parts(length).reshape(length, 2, chips, 2, kk).transpose(2, 0, 3, 1, 4)
    table = jnp.asarray(table.reshape(chips, length, 2 * lanes), jnp.bfloat16)
    mine = lax.dynamic_slice_in_dim(delay_table.T, lax.axis_index("beam") * kk, kk, axis=1)
    delays = jnp.tile(mine, (1, frames))
    rows = curves * frames
    chunks = frames // CHUNK
    bf16, f32 = jnp.bfloat16, jnp.float32
    vmem = pl.BlockSpec(memory_space=pltpu.VMEM)
    flops = 2 * inputs * frames * length * length + 8 * 2 * frames * kk * stations * beams * 2
    summed = pl.pallas_call(
        functools.partial(kernel, chips, frames),
        out_shape=jax.ShapeDtypeStruct((rows, 128), f32),
        in_specs=[vmem] * 6,
        out_specs=vmem,
        scratch_shapes=[
            pltpu.VMEM((inputs, (tap_count - 1) * length), bf16),
            pltpu.VMEM((CHUNK, inputs, 128), f32),
            pltpu.VMEM((CHUNK, 2, inputs // 2, length), bf16),
            pltpu.VMEM((chunks, chips, 2, CHUNK, 2, inputs // 2, lanes), bf16),
            pltpu.VMEM((frames, 2, 2 * chips, inputs // 2, lanes), bf16),
            pltpu.VMEM((2, CHUNK * lanes, stations), bf16),
            pltpu.VMEM((2, stations, 2 * beams), bf16),
            pltpu.VMEM((frames, kk, beams), f32),
            pltpu.VMEM((frames * kk, beams), bf16),
            pltpu.VMEM((4 * kk, beams), bf16),
            pltpu.VMEM((2 * rows, frames * kk), bf16),
            pltpu.VMEM((2 * rows, 4 * kk), bf16),
            pltpu.VMEM((2, chips, 2, rows, 128), f32),
            pltpu.VMEM((chips, 2, rows, 128), f32),
            pltpu.VMEM((chips, 2, rows, 128), f32),
            pltpu.VMEM((chips, rows, 128), f32),
            pltpu.VMEM((chips, rows, 128), f32),
            pltpu.VMEM((chips, rows, 128), f32),
            pltpu.SemaphoreType.DMA((2,)),
            pltpu.SemaphoreType.DMA((chunks, chips, 2)),
            pltpu.SemaphoreType.DMA((chunks, chips, 2)),
            pltpu.SemaphoreType.DMA((3, chips)),
            pltpu.SemaphoreType.DMA((3, chips)),
        ],
        compiler_params=pltpu.CompilerParams(
            collective_id=0, has_side_effects=True, vmem_limit_bytes=48 * 2**20
        ),
        cost_estimate=pl.CostEstimate(flops=flops, bytes_accessed=2**23, transcendentals=0),
    )(
        voltages,
        filter_taps,
        table,
        beam_weights.reshape(stations, 2 * beams),
        station_index.reshape(stations, 2),
        delays,
    )
    return jnp.transpose(summed.reshape(curves, frames, 128), (2, 0, 1))


def shards(voltages, filter_taps, beam_weights, station_index, delay_table):
    length = filter_taps.shape[1]
    frames = voltages.shape[1] // length
    chips, cores = lax.axis_size("chan"), lax.axis_size("beam")
    fits = (
        lax.axis_size("tm") == 2
        and cores == 2
        and delay_table.shape[0] == 128
        and frames % 16 == 0
        and voltages.shape[0] % 32 == 0
        and length % 128 == 0
        and beam_weights.shape[2] == chips * cores * 128
        and filter_taps.shape[0] - 1 <= frames
        and frames - 2 * CHUNK >= filter_taps.shape[0] - 1
    )
    form = kernel_shards if fits else collective_shards
    return form(voltages, filter_taps, beam_weights, station_index, delay_table)


def solution(mesh):
    in_specs = (P(("groups", "chan", "beam"), "tm"), P(), P(), P(), P("chan", None))
    out_specs = P(("groups", "chan", "beam"), None, "tm")
    return jax.shard_map(shards, mesh=mesh, in_specs=in_specs, out_specs=out_specs, check_vma=False)
```
